32 devices in a mesh: cd: 8 (over z, y), ab: 4 (over x, core).
Axes of the slice: x: 2, y: 2, z: 4, core: 2. Of those that a mesh axis runs over, the one named last changes fastest.
Arguments:
- amplitudes: bfloat16 [512, 8, 800], P('cd', None, 'ab'), may hold values from -6 to 6
- integrals: bfloat16 [8, 800, 2048], P('cd', None, 'ab'), may hold values from -0.078125 to 0.078125
Outputs:
- ladder: float32 [512, 2048], P('cd', 'ab')
The draws below stay inside these ranges and needn't reach their ends.
All inputs are finite; a program needn't handle non-finite values.
Results may differ from the reference program's by a relative error of at most 0.0003.
Values may be sent and summed in bfloat16 or wider, within the bound.
A program may use at most 64 MiB of HBM per device.

```python
import jax
import jax.numpy as jnp

NPAIR = 512
DV = 800
CV = 8
AB = 2048


def steps_of(key, dims, shards, least, top_value):
    def one(dim, shards_of):
        draws = jax.random.uniform(jax.random.fold_in(jax.random.fold_in(key, 6), dim), (shards_of,), jnp.float32, least / len(shards), top_value / len(shards))
        return jnp.repeat(jnp.exp(draws), dims[dim] // shards_of).reshape((-1,) + (1,) * (len(dims) - dim - 1))

    gain = one(*shards[0])
    for cut in shards[1:]:
        gain = gain * one(*cut)
    return gain


def gaussian(key, extent, deviation, most, pieces=(), held_as=jnp.bfloat16):
    drawn = deviation * jax.random.normal(key, extent, jnp.float32)
    if pieces:
        drawn = drawn * steps_of(key, extent, pieces, -0.22, 0.18)
    return jnp.clip(drawn, -most, most).astype(held_as)


def setup_inputs(seed: int = 0) -> dict:
    key_of = jax.random.split(jax.random.key(seed), 3)
    return {
        "amplitudes": gaussian(key_of[0], (NPAIR, CV, DV), 1.0, 6.0, ((0, 8), (2, 4))),
        "integrals": gaussian(key_of[1], (CV, DV, AB), (CV * DV) ** -0.5, 0.078125, ((0, 8), (2, 4))),
    }


def reference(amplitudes, integrals):
    pairs = amplitudes.reshape(amplitudes.shape[0], amplitudes.shape[1] * amplitudes.shape[2])
    slab = integrals.reshape(integrals.shape[0] * integrals.shape[1], integrals.shape[2])
    return jnp.dot(pairs, slab, preferred_element_type=jnp.float32)
```

```python
import functools

import jax
import jax.numpy as jnp
from jax import lax
from jax.experimental import pallas as pl
from jax.experimental.pallas import tpu as pltpu
from jax.sharding import PartitionSpec as P

MESH = pl.DeviceIdType.MESH
LANES = 128
FAR = (1, 3, 2)
PLAN = (
("a", 1), ("l", 0), ("r", 0), ("a", 3), ("a", 2), ("r", 1), ("p", 0), ("r", 3), ("r", 2), ("p", 1), ("y", 0), ("f", (1, 0)), ("p", 3), ("f", (3, 0)), ("p", 2), ("f", (2, 0)), ("f", (0, 0)),("y", 1), ("f", (3, 1)), ("f", (2, 1)), ("f", (1, 1)), ("f", (0, 1)), ("y", 2), ("f", (3, 2)), ("f", (2, 2)), ("f", (1, 2)), ("f", (0, 2)), ("y", 3), ("f", (3, 3)), ("f", (2, 3)), ("f", (1, 3)), ("f", (0, 3)),
)


def flip(index, bits):
    out = index
    bit = 1
    while bit <= bits:
        if bits & bit:
            out = out + bit - 2 * bit * (lax.div(index, bit) % 2)
        bit *= 2
    return out


def kernel(
    amp_ref, int_ref, part_ref, stage, held, slab, acc, amp, mine, other,
    sent, a_r, x_r, c_r, y_r, z_r, local_sem,
):
    cd = lax.axis_index("cd")
    ab = lax.axis_index("ab")
    rows, n_cd, width = amp_ref.shape
    wide = stage.shape[2]
    n_ab = slab.shape[1]
    n_z = held.shape[1]
    columns = int_ref.shape[1]
    pieces = columns // LANES
    both = (0, 1)

    load_amp = pltpu.make_async_copy(amp_ref, amp, local_sem.at[0])
    load_int = pltpu.make_async_copy(int_ref, mine, local_sem.at[1])
    load_amp.start()
    load_int.start()
    peers = [(flip(cd, k), ab) for k in (1, 2, 4, 6)]
    peers += [(cd, flip(ab, 1)), (cd, flip(ab, 2))]
    barrier = pltpu.get_barrier_semaphore()
    for peer in peers:
        pl.semaphore_signal(barrier, inc=1, device_id=peer, device_id_type=MESH)

    stage[:, :, width:] = jnp.zeros((n_cd, rows, wide - width), stage.dtype)
    load_amp.wait()
    for c in range(n_cd):
        stage[c, :, :width] = amp[:, c, :]
    for s in both:
        held[0, 0, s] = stage[flip(cd, s)]

    pl.semaphore_wait(barrier, len(peers))

    def remote(src, dst, s, r, peer):
        return pltpu.make_async_remote_copy(
            src_ref=src, dst_ref=dst, send_sem=s, recv_sem=r,
            device_id=peer, device_id_type=MESH,
        )

    def whole(like, sem):
        pltpu.make_async_copy(like, like, sem).wait()

    def cols(q):
        return pl.ds(q * LANES, LANES)

    acopy = {
        (k, s): remote(
            stage.at[flip(cd, 2 * k + s)], held.at[0, k, s], sent.at[0], a_r.at[k, s], (flip(cd, 2 * k), ab)
        )
        for k in FAR
        for s in both
    }
    xcopy = {
        (k, s): remote(held.at[0, k, s], held.at[2, k, s], sent.at[1], x_r.at[k, s], (cd, flip(ab, 2)))
        for k in range(n_z)
        for s in both
    }
    ccopy = {
        (r, k, s): remote(
            held.at[r, k, s], held.at[r + 1, k, s], sent.at[2], c_r.at[k], (cd, flip(ab, 1))
        )
        for r in (0, 2)
        for k in range(n_z)
        for s in both
    }
    ycopy = {
        q: remote(int_ref.at[:, cols(q)], other.at[:, cols(q)], sent.at[3], y_r.at[q], (flip(cd, 1), ab))
        for q in range(pieces)
    }
    zcopy = {
        (k, q): remote(acc.at[k, :, cols(q)], part_ref.at[k, :, cols(q)], sent.at[4], z_r.at[0], (flip(cd, 2 * k), ab))
        for k in FAR
        for q in range(pieces)
    }
    for s in both:
        xcopy[0, s].start()
        ccopy[0, 0, s].start()
    for k in FAR:
        for s in both:
            acopy[k, s].start()
    core = lax.rem(ab, 2)

    @pl.when(core == 0)
    def _():
        for q in range(pieces):
            ycopy[q].start()


    load_int.wait()
    for s in both:
        slab[s, :, width:, :] = jnp.zeros((n_ab, wide - width, columns), slab.dtype)
    for j in range(n_ab):
        slab[0, j, :width, :] = mine[j * width : (j + 1) * width, :]

    def arrive(k):
        for s in both:
            acopy[k, s].wait_recv()
            xcopy[k, s].start()
            ccopy[0, k, s].start()

    def relay(k):
        for s in both:
            xcopy[k, s].wait_recv()
            ccopy[2, k, s].start()

    def product(k):
        whole(held.at[0:2, k], c_r.at[k])
        total = jnp.dot(held[0, k, 0], slab[0, ab], preferred_element_type=jnp.float32)
        for r in range(1, n_ab):
            total += jnp.dot(held[r, k, 0], slab[0, flip(ab, r)], preferred_element_type=jnp.float32)
        acc[k] = total

    def piece(q):
        ycopy[q].wait_recv()
        here = slice(q * LANES, (q + 1) * LANES)
        for j in range(n_ab):
            slab[1, j, :width, here] = other[j * width : (j + 1) * width, here]

    def finish(kq):
        k, q = kq
        here = slice(q * LANES, (q + 1) * LANES)
        total = acc[k, :, here]
        for r in range(n_ab):
            total += jnp.dot(held[r, k, 1], slab[1, flip(ab, r), :, here], preferred_element_type=jnp.float32)
        acc[k, :, here] = total
        if k:
            zcopy[k, q].start()

    def late(k):
        @pl.when(core == 1)
        def _():
            for q in range(pieces):
                ycopy[q].start()

    act = {"l": late, "a": arrive, "r": relay, "p": product, "y": piece, "f": finish}
    for what, k in PLAN:
        act[what](k)
    own = pltpu.make_async_copy(acc.at[0], part_ref.at[0], local_sem.at[2])
    own.start()
    own.wait()
    whole(held.at[0, 1:], sent.at[0])
    whole(held.at[0], sent.at[1])
    whole(held.at[0:2], sent.at[2])
    whole(other, sent.at[3])
    whole(acc.at[1:], sent.at[4])
    whole(acc.at[1:], z_r.at[0])


def by_kernel(amplitudes, integrals, n_ab):
    rows, n_cd, width = amplitudes.shape
    columns = integrals.shape[2]
    wide = -(-width // LANES) * LANES
    n_z = n_cd // 2
    pieces = columns // LANES
    dma = pltpu.SemaphoreType.DMA
    parts = pl.pallas_call(
        kernel,
        out_shape=jax.ShapeDtypeStruct((n_z, rows, columns), jnp.float32),
        in_specs=[pl.BlockSpec(memory_space=pltpu.HBM)] * 2,
        out_specs=pl.BlockSpec(memory_space=pltpu.HBM),
        scratch_shapes=[
            pltpu.VMEM((n_cd, rows, wide), amplitudes.dtype),
            pltpu.VMEM((n_ab, n_z, 2, rows, wide), amplitudes.dtype),
            pltpu.VMEM((2, n_ab, wide, columns), integrals.dtype),
            pltpu.VMEM((n_z, rows, columns), jnp.float32),
            pltpu.VMEM(amplitudes.shape, amplitudes.dtype),
            pltpu.VMEM(integrals.shape[1:], integrals.dtype),
            pltpu.VMEM(integrals.shape[1:], integrals.dtype),
            dma((5,)), dma((n_z, 2)), dma((n_z, 2)), dma((n_z,)), dma((pieces,)), dma((1,)),
            dma((3,)),
        ],
        compiler_params=pltpu.CompilerParams(
            collective_id=0, has_side_effects=True, vmem_limit_bytes=56 * 1024 * 1024
        ),
    )(amplitudes, integrals.reshape(integrals.shape[1], columns))
    return jnp.sum(parts, axis=0)


def by_collectives(amplitudes, integrals):
    c_local, depth, columns = integrals.shape
    mine = lax.all_to_all(amplitudes, "cd", split_axis=1, concat_axis=0, tiled=True)
    complete = lax.all_gather(mine, "ab", axis=2, tiled=True)
    flat = complete.reshape(complete.shape[0], c_local * depth)
    slab = integrals.reshape(c_local * depth, columns)
    partial = jnp.dot(flat, slab, preferred_element_type=jnp.float32)
    return lax.psum_scatter(partial, "cd", scatter_dimension=0, tiled=True)


def on_device(n_cd, n_ab, amplitudes, integrals):
    rows = amplitudes.shape[0]
    columns = integrals.shape[2]
    if n_cd == 8 and n_ab == 4 and integrals.shape[0] == 1 and rows % 16 == 0 and columns % LANES == 0:
        return by_kernel(amplitudes, integrals, n_ab)
    return by_collectives(amplitudes, integrals)


def solution(mesh):
    specs = (P("cd", None, "ab"), P("cd", None, "ab"))
    return jax.shard_map(
        functools.partial(on_device, mesh.shape["cd"], mesh.shape["ab"]),
        mesh=mesh, in_specs=specs, out_specs=P("cd", "ab"), check_vma=False,
    )
```

```python
import functools

import jax
import jax.numpy as jnp
from jax import lax
from jax.experimental import pallas as pl
from jax.experimental.pallas import tpu as pltpu
from jax.sharding import PartitionSpec as P

MESH = pl.DeviceIdType.MESH
LANES = 128
FAR = (1, 3, 2)
PLAN = (
("a", 1), ("l", 0), ("r", 0), ("a", 3), ("a", 2), ("r", 1), ("p", 0), ("r", 3), ("r", 2), ("p", 1), ("y", 0), ("f", (1, 0)), ("p", 3), ("f", (3, 0)), ("p", 2), ("f", (2, 0)), ("f", (0, 0)),("y", 1), ("f", (3, 1)), ("f", (2, 1)), ("f", (1, 1)), ("f", (0, 1)), ("y", 2), ("f", (3, 2)), ("f", (2, 2)), ("f", (1, 2)), ("f", (0, 2)), ("y", 3), ("f", (3, 3)), ("f", (2, 3)), ("f", (1, 3)), ("f", (0, 3)),
)


def flip(index, bits):
    out = index
    bit = 1
    while bit <= bits:
        if bits & bit:
            out = out + bit - 2 * bit * (lax.div(index, bit) % 2)
        bit *= 2
    return out


def kernel(
    amp_ref, int_ref, part_ref, stage, held, slab, acc, amp, mine, other,
    sent, a_r, x_r, c_r, y_r, z_r, local_sem,
):
    cd = lax.axis_index("cd")
    ab = lax.axis_index("ab")
    rows, n_cd, width = amp_ref.shape
    wide = stage.shape[2]
    n_ab = slab.shape[1]
    n_z = held.shape[1]
    columns = int_ref.shape[1]
    pieces = columns // LANES
    both = (0, 1)

    load_amp = pltpu.make_async_copy(amp_ref, amp, local_sem.at[0])
    load_int = pltpu.make_async_copy(int_ref, mine, local_sem.at[1])
    load_amp.start()
    load_int.start()
    peers = [(flip(cd, k), ab) for k in (1, 2, 4, 6)]
    peers += [(cd, flip(ab, 1)), (cd, flip(ab, 2))]
    barrier = pltpu.get_barrier_semaphore()
    for peer in peers:
        pl.semaphore_signal(barrier, inc=1, device_id=peer, device_id_type=MESH)

    stage[:, :, width:] = jnp.zeros((n_cd, rows, wide - width), stage.dtype)
    load_amp.wait()
    for c in range(n_cd):
        stage[c, :, :width] = amp[:, c, :]
    for s in both:
        held[0, 0, s] = stage[flip(cd, s)]

    pl.semaphore_wait(barrier, len(peers))

    def remote(src, dst, s, r, peer):
        return pltpu.make_async_remote_copy(
            src_ref=src, dst_ref=dst, send_sem=s, recv_sem=r,
            device_id=peer, device_id_type=MESH,
        )

    def whole(like, sem):
        pltpu.make_async_copy(like, like, sem).wait()

    def sums(k):
        return acc.at[k] if k else part_ref.at[0]

    def cols(q):
        return pl.ds(q * LANES, LANES)

    acopy = {
        (k, s): remote(
            stage.at[flip(cd, 2 * k + s)], held.at[0, k, s], sent.at[0], a_r.at[k, s], (flip(cd, 2 * k), ab)
        )
        for k in FAR
        for s in both
    }
    xcopy = {
        (k, s): remote(held.at[0, k, s], held.at[2, k, s], sent.at[1], x_r.at[k, s], (cd, flip(ab, 2)))
        for k in range(n_z)
        for s in both
    }
    ccopy = {
        (r, k, s): remote(
            held.at[r, k, s], held.at[r + 1, k, s], sent.at[2], c_r.at[k], (cd, flip(ab, 1))
        )
        for r in (0, 2)
        for k in range(n_z)
        for s in both
    }
    ycopy = {
        q: remote(mine.at[:, cols(q)], other.at[:, cols(q)], sent.at[3], y_r.at[q], (flip(cd, 1), ab))
        for q in range(pieces)
    }
    zcopy = {
        (k, q): remote(acc.at[k, :, cols(q)], part_ref.at[k, :, cols(q)], sent.at[4], z_r.at[0], (flip(cd, 2 * k), ab))
        for k in FAR
        for q in range(pieces)
    }
    for s in both:
        xcopy[0, s].start()
        ccopy[0, 0, s].start()
    for k in FAR:
        for s in both:
            acopy[k, s].start()
    core = lax.rem(ab, 2)

    load_int.wait()

    @pl.when(core == 0)
    def _():
        for q in range(pieces):
            ycopy[q].start()


    for s in both:
        slab[s, :, width:, :] = jnp.zeros((n_ab, wide - width, columns), slab.dtype)
    for j in range(n_ab):
        slab[0, j, :width, :] = mine[j * width : (j + 1) * width, :]

    def arrive(k):
        for s in both:
            acopy[k, s].wait_recv()
            xcopy[k, s].start()
            ccopy[0, k, s].start()

    def relay(k):
        for s in both:
            xcopy[k, s].wait_recv()
            ccopy[2, k, s].start()

    def product(k):
        whole(held.at[0:2, k], c_r.at[k])
        total = jnp.dot(held[0, k, 0], slab[0, ab], preferred_element_type=jnp.float32)
        for r in range(1, n_ab):
            total += jnp.dot(held[r, k, 0], slab[0, flip(ab, r)], preferred_element_type=jnp.float32)
        sums(k)[...] = total

    def piece(q):
        ycopy[q].wait_recv()
        here = slice(q * LANES, (q + 1) * LANES)
        for j in range(n_ab):
            slab[1, j, :width, here] = other[j * width : (j + 1) * width, here]

    def finish(kq):
        k, q = kq
        here = slice(q * LANES, (q + 1) * LANES)
        total = sums(k)[:, here]
        for r in range(n_ab):
            total += jnp.dot(held[r, k, 1], slab[1, flip(ab, r), :, here], preferred_element_type=jnp.float32)
        sums(k)[:, here] = total
        if k:
            zcopy[k, q].start()

    def late(k):
        @pl.when(core == 1)
        def _():
            for q in range(pieces):
                ycopy[q].start()

    act = {"l": late, "a": arrive, "r": relay, "p": product, "y": piece, "f": finish}
    for what, k in PLAN:
        act[what](k)
    whole(held.at[0, 1:], sent.at[0])
    whole(held.at[0], sent.at[1])
    whole(held.at[0:2], sent.at[2])
    whole(other, sent.at[3])
    whole(acc.at[1:], sent.at[4])
    whole(acc.at[1:], z_r.at[0])


def by_kernel(amplitudes, integrals, n_ab):
    rows, n_cd, width = amplitudes.shape
    columns = integrals.shape[2]
    wide = -(-width // LANES) * LANES
    n_z = n_cd // 2
    pieces = columns // LANES
    dma = pltpu.SemaphoreType.DMA
    parts = pl.pallas_call(
        kernel,
        out_shape=pltpu.VMEM((n_z, rows, columns), jnp.float32),
        in_specs=[pl.BlockSpec(memory_space=pltpu.HBM)] * 2,
        out_specs=pl.BlockSpec(memory_space=pltpu.VMEM),
        scratch_shapes=[
            pltpu.VMEM((n_cd, rows, wide), amplitudes.dtype),
            pltpu.VMEM((n_ab, n_z, 2, rows, wide), amplitudes.dtype),
            pltpu.VMEM((2, n_ab, wide, columns), integrals.dtype),
            pltpu.VMEM((n_z, rows, columns), jnp.float32),
            pltpu.VMEM(amplitudes.shape, amplitudes.dtype),
            pltpu.VMEM(integrals.shape[1:], integrals.dtype),
            pltpu.VMEM(integrals.shape[1:], integrals.dtype),
            dma((5,)), dma((n_z, 2)), dma((n_z, 2)), dma((n_z,)), dma((pieces,)), dma((1,)),
            dma((2,)),
        ],
        compiler_params=pltpu.CompilerParams(
            collective_id=0, has_side_effects=True, vmem_limit_bytes=32 * 1024 * 1024
        ),
    )(
        pltpu.with_memory_space_constraint(amplitudes, pltpu.HBM),
        pltpu.with_memory_space_constraint(integrals.reshape(integrals.shape[1], columns), pltpu.HBM),
    )
    return jnp.sum(parts, axis=0)


def by_collectives(amplitudes, integrals):
    c_local, depth, columns = integrals.shape
    mine = lax.all_to_all(amplitudes, "cd", split_axis=1, concat_axis=0, tiled=True)
    complete = lax.all_gather(mine, "ab", axis=2, tiled=True)
    flat = complete.reshape(complete.shape[0], c_local * depth)
    slab = integrals.reshape(c_local * depth, columns)
    partial = jnp.dot(flat, slab, preferred_element_type=jnp.float32)
    return lax.psum_scatter(partial, "cd", scatter_dimension=0, tiled=True)


def on_device(n_cd, n_ab, amplitudes, integrals):
    rows = amplitudes.shape[0]
    columns = integrals.shape[2]
    if n_cd == 8 and n_ab == 4 and integrals.shape[0] == 1 and rows % 16 == 0 and columns % LANES == 0:
        return by_kernel(amplitudes, integrals, n_ab)
    return by_collectives(amplitudes, integrals)


def solution(mesh):
    specs = (P("cd", None, "ab"), P("cd", None, "ab"))
    return jax.shard_map(
        functools.partial(on_device, mesh.shape["cd"], mesh.shape["ab"]),
        mesh=mesh, in_specs=specs, out_specs=P("cd", "ab"), check_vma=False,
    )
```

```python
import functools

import jax
import jax.numpy as jnp
from jax import lax
from jax.experimental import pallas as pl
from jax.experimental.pallas import tpu as pltpu
from jax.sharding import PartitionSpec as P

MESH = pl.DeviceIdType.MESH
LANES = 128
VIA = 1
FAR = (1, 3, 2)
PLAN = (
    ("a", 1), ("a", 3), ("r", 0), ("r", 1), ("a", 2), ("p", 1), ("y", 0), ("f", (1, 0)), ("r", 3), ("p", 0), ("r", 2), ("p", 3), ("f", (3, 0)), ("p", 2), ("f", (2, 0)), ("y", 1), ("f", (3, 1)), ("f", (2, 1)), ("f", (1, 1)), ("f", (0, 0)), ("f", (0, 1)), ("h", 0), ("y", 2), ("f", (3, 2)), ("f", (2, 2)), ("f", (1, 2)), ("f", (0, 2)), ("y", 3), ("f", (3, 3)), ("f", (2, 3)), ("f", (1, 3)), ("f", (0, 3)),
)


def flip(index, bits):
    out = index
    bit = 1
    while bit <= bits:
        if bits & bit:
            out = out + bit - 2 * bit * (lax.div(index, bit) % 2)
        bit *= 2
    return out


def kernel(
    amp_ref, int_ref, part_ref, stage, held, slab, acc, amp, mine, other, lent,
    sent, a_r, x_r, c_r, y_r, l_r, z_r, h_r, near, local_sem,
):
    cd = lax.axis_index("cd")
    ab = lax.axis_index("ab")
    rows, n_cd, width = amp_ref.shape
    wide = stage.shape[2]
    n_ab = slab.shape[1]
    n_z = held.shape[1]
    columns = int_ref.shape[1]
    pieces = columns // LANES
    both = (0, 1)

    load_amp = pltpu.make_async_copy(amp_ref, amp, local_sem.at[0])
    load_int = [
        pltpu.make_async_copy(int_ref.at[:, pl.ds(q * LANES, LANES)], mine.at[q], local_sem.at[1])
        for q in range(pieces)
    ]
    load_amp.start()
    for q in range(pieces):
        load_int[q].start()
    peers = [(flip(cd, k), ab) for k in (1, 2, 4, 6)]
    peers += [(cd, flip(ab, 1)), (cd, flip(ab, 2)), (flip(cd, 1), flip(ab, 1))]
    barrier = pltpu.get_barrier_semaphore()
    for peer in peers:
        pl.semaphore_signal(barrier, inc=1, device_id=peer, device_id_type=MESH)

    stage[:, :, width:] = jnp.zeros((n_cd, rows, wide - width), stage.dtype)
    load_amp.wait()
    for c in range(n_cd):
        stage[c, :, :width] = amp[:, c, :]
    for s in both:
        held[0, 0, s] = stage[flip(cd, s)]

    pl.semaphore_wait(barrier, len(peers))

    def remote(src, dst, s, r, peer):
        return pltpu.make_async_remote_copy(
            src_ref=src, dst_ref=dst, send_sem=s, recv_sem=r,
            device_id=peer, device_id_type=MESH,
        )

    def whole(like, sem):
        pltpu.make_async_copy(like, like, sem).wait()

    def sums(k):
        return acc.at[k] if k else part_ref.at[0]

    def cols(q):
        return pl.ds(q * LANES, LANES)

    acopy = {
        (k, s): remote(
            stage.at[flip(cd, 2 * k + s)], held.at[0, k, s], sent.at[0], a_r.at[k, s], (flip(cd, 2 * k), ab)
        )
        for k in FAR
        for s in both
    }
    xcopy = {
        (k, s): remote(held.at[0, k, s], held.at[2, k, s], sent.at[1], x_r.at[k, s], (cd, flip(ab, 2)))
        for k in range(n_z)
        for s in both
    }
    ccopy = {
        (r, k, s): remote(
            held.at[r, k, s], held.at[r + 1, k, s], sent.at[2], c_r.at[k], (cd, flip(ab, 1))
        )
        for r in (0, 2)
        for k in range(n_z)
        for s in both
    }
    deep = lent.shape[1]
    lend = {
        q: remote(mine.at[q, deep:], lent.at[q], sent.at[7], l_r.at[q], (cd, flip(ab, 1)))
        for q in range(pieces)
    }
    ycopy = {
        q: remote(mine.at[q, :deep], other.at[q, :deep], sent.at[3], y_r.at[q], (flip(cd, 1), ab))
        for q in range(pieces)
    }
    lcopy = {
        q: remote(lent.at[q], other.at[q, deep:], sent.at[3], y_r.at[q], (flip(cd, 1), flip(ab, 1)))
        for q in range(pieces)
    }
    zcopy = {
        (k, q): remote(
            acc.at[k, :, cols(q)], part_ref.at[k, :, cols(q)], sent.at[3 + k], z_r.at[k], (flip(cd, 2 * k), ab)
        )
        for k in FAR
        for q in range(pieces)
        if k < 3 or q >= VIA
    }
    hcopy = {
        q: remote(acc.at[3, :, cols(q)], near.at[q], sent.at[8], h_r.at[q], (flip(cd, 2), ab)) for q in range(VIA)
    }
    for s in both:
        xcopy[0, s].start()
        ccopy[0, 0, s].start()
    for k in FAR:
        for s in both:
            acopy[k, s].start()
    core = lax.rem(ab, 2)
    whole(mine, local_sem.at[1])
    ycopy[0].start()
    for q in range(pieces):
        lend[q].start()

    @pl.when(core == 0)
    def _():
        for q in range(pieces):
            if q:
                ycopy[q].start()
            lend[q].wait_recv()
            lcopy[q].start()

    @pl.when(core == 1)
    def _():
        for q in range(pieces):
            lend[q].wait_recv()
            lcopy[q].start()
            if q:
                ycopy[q].start()

    for s in both:
        slab[s, :, width:, :] = jnp.zeros((n_ab, wide - width, columns), slab.dtype)
    for j in range(n_ab):
        for q in range(pieces):
            slab[0, j, :width, q * LANES : (q + 1) * LANES] = mine[q, j * width : (j + 1) * width, :]

    def arrive(k):
        for s in both:
            acopy[k, s].wait_recv()
            xcopy[k, s].start()
            ccopy[0, k, s].start()

    def relay(k):
        for s in both:
            xcopy[k, s].wait_recv()
            ccopy[2, k, s].start()

    def product(k):
        whole(held.at[0:2, k], c_r.at[k])
        total = jnp.dot(held[0, k, 0], slab[0, ab], preferred_element_type=jnp.float32)
        for r in range(1, n_ab):
            total += jnp.dot(held[r, k, 0], slab[0, flip(ab, r)], preferred_element_type=jnp.float32)
        sums(k)[...] = total

    def piece(q):
        whole(other.at[q], y_r.at[q])
        here = slice(q * LANES, (q + 1) * LANES)
        for j in range(n_ab):
            slab[1, j, :width, here] = other[q, j * width : (j + 1) * width, :]

    def finish(kq):
        k, q = kq
        here = slice(q * LANES, (q + 1) * LANES)
        total = sums(k)[:, here]
        for r in range(n_ab):
            total += jnp.dot(held[r, k, 1], slab[1, flip(ab, r), :, here], preferred_element_type=jnp.float32)
        sums(k)[:, here] = total
        if k == 3 and q < VIA:
            hcopy[q].start()
        elif k == 1 or k and q >= VIA:
            zcopy[k, q].start()

    def pass_on(q):
        h = slice(q * LANES, (q + 1) * LANES)
        hcopy[q].wait_recv()
        acc[2, :, h] += near[q]
        zcopy[2, q].start()

    part_ref[3, :, : VIA * LANES] = jnp.zeros((rows, VIA * LANES), part_ref.dtype)
    act = {"a": arrive, "r": relay, "p": product, "y": piece, "f": finish, "h": pass_on}
    for what, k in PLAN:
        act[what](k)
    whole(held.at[0, 1:], sent.at[0])
    whole(near, sent.at[8])
    whole(held.at[0], sent.at[1])
    whole(held.at[0:2], sent.at[2])
    whole(other, sent.at[3])
    whole(lent, sent.at[7])
    for k in FAR:
        direct = acc.at[k, :, VIA * LANES :] if k == 3 else acc.at[k]
        whole(direct, sent.at[3 + k])
        whole(direct, z_r.at[k])


def by_kernel(amplitudes, integrals, n_ab):
    rows, n_cd, width = amplitudes.shape
    columns = integrals.shape[2]
    wide = -(-width // LANES) * LANES
    n_z = n_cd // 2
    pieces = columns // LANES
    dma = pltpu.SemaphoreType.DMA
    parts = pl.pallas_call(
        kernel,
        out_shape=pltpu.VMEM((n_z, rows, columns), jnp.float32),
        in_specs=[pl.BlockSpec(memory_space=pltpu.HBM)] * 2,
        out_specs=pl.BlockSpec(memory_space=pltpu.VMEM),
        scratch_shapes=[
            pltpu.VMEM((n_cd, rows, wide), amplitudes.dtype),
            pltpu.VMEM((n_ab, n_z, 2, rows, wide), amplitudes.dtype),
            pltpu.VMEM((2, n_ab, wide, columns), integrals.dtype),
            pltpu.VMEM((n_z, rows, columns), jnp.float32),
            pltpu.VMEM(amplitudes.shape, amplitudes.dtype),
            pltpu.VMEM((pieces, integrals.shape[1], LANES), integrals.dtype),
            pltpu.VMEM((pieces, integrals.shape[1], LANES), integrals.dtype),
            pltpu.VMEM((pieces, integrals.shape[1] // 2, LANES), integrals.dtype),
            dma((9,)), dma((n_z, 2)), dma((n_z, 2)), dma((n_z,)), dma((pieces,)), dma((pieces,)), dma((n_z,)), dma((VIA,)), pltpu.VMEM((VIA, rows, LANES), jnp.float32),
            dma((2,)),
        ],
        compiler_params=pltpu.CompilerParams(
            collective_id=0, has_side_effects=True, vmem_limit_bytes=32 * 1024 * 1024
        ),
    )(
        pltpu.with_memory_space_constraint(amplitudes, pltpu.HBM),
        pltpu.with_memory_space_constraint(integrals.reshape(integrals.shape[1], columns), pltpu.HBM),
    )
    return jnp.sum(parts, axis=0)


def by_collectives(amplitudes, integrals):
    c_local, depth, columns = integrals.shape
    mine = lax.all_to_all(amplitudes, "cd", split_axis=1, concat_axis=0, tiled=True)
    complete = lax.all_gather(mine, "ab", axis=2, tiled=True)
    flat = complete.reshape(complete.shape[0], c_local * depth)
    slab = integrals.reshape(c_local * depth, columns)
    partial = jnp.dot(flat, slab, preferred_element_type=jnp.float32)
    return lax.psum_scatter(partial, "cd", scatter_dimension=0, tiled=True)


def on_device(n_cd, n_ab, amplitudes, integrals):
    rows = amplitudes.shape[0]
    columns = integrals.shape[2]
    if n_cd == 8 and n_ab == 4 and integrals.shape[0] == 1 and rows % 16 == 0 and columns % LANES == 0 and integrals.shape[1] % 32 == 0:
        return by_kernel(amplitudes, integrals, n_ab)
    return by_collectives(amplitudes, integrals)


def solution(mesh):
    specs = (P("cd", None, "ab"), P("cd", None, "ab"))
    return jax.shard_map(
        functools.partial(on_device, mesh.shape["cd"], mesh.shape["ab"]),
        mesh=mesh, in_specs=specs, out_specs=P("cd", "ab"), check_vma=False,
    )
```

```python
import functools

import jax
import jax.numpy as jnp
from jax import lax
from jax.experimental import pallas as pl
from jax.experimental.pallas import tpu as pltpu
from jax.sharding import PartitionSpec as P

MESH = pl.DeviceIdType.MESH
LANES = 128
VIA = 1
FAR = (1, 3, 2)
PLAN = (
    ("a", 1), ("a", 3), ("r", 0), ("r", 1), ("a", 2), ("p", 1), ("y", 0), ("f", (1, 0)), ("r", 3), ("p", 0), ("r", 2), ("p", 3), ("f", (3, 0)), ("p", 2), ("f", (2, 0)), ("y", 1), ("f", (3, 1)), ("f", (2, 1)), ("f", (1, 1)), ("f", (0, 0)), ("f", (0, 1)), ("i", 0), ("y", 2), ("f", (3, 2)), ("f", (2, 2)), ("f", (1, 2)), ("f", (0, 2)), ("j", 0), ("y", 3), ("f", (3, 3)), ("f", (2, 3)), ("f", (1, 3)), ("f", (0, 3)),
)


def flip(index, bits):
    out = index
    bit = 1
    while bit <= bits:
        if bits & bit:
            out = out + bit - 2 * bit * (lax.div(index, bit) % 2)
        bit *= 2
    return out


def kernel(
    amp_ref, int_ref, part_ref, stage, held, slab, acc, amp, mine, other, lent,
    sent, a_r, x_r, c_r, y_r, l_r, z_r, h_r, near, local_sem,
):
    cd = lax.axis_index("cd")
    ab = lax.axis_index("ab")
    rows, n_cd, width = amp_ref.shape
    wide = stage.shape[2]
    n_ab = slab.shape[1]
    n_z = held.shape[1]
    columns = int_ref.shape[1]
    pieces = columns // LANES
    both = (0, 1)

    load_amp = pltpu.make_async_copy(amp_ref, amp, local_sem.at[0])
    load_int = [
        pltpu.make_async_copy(int_ref.at[:, pl.ds(q * LANES, LANES)], mine.at[q], local_sem.at[1])
        for q in range(pieces)
    ]
    load_amp.start()
    for q in range(pieces):
        load_int[q].start()
    peers = [(flip(cd, k), ab) for k in (1, 2, 4, 6)]
    peers += [(cd, flip(ab, 1)), (cd, flip(ab, 2)), (flip(cd, 1), flip(ab, 1))]
    barrier = pltpu.get_barrier_semaphore()
    for peer in peers:
        pl.semaphore_signal(barrier, inc=1, device_id=peer, device_id_type=MESH)

    stage[:, :, width:] = jnp.zeros((n_cd, rows, wide - width), stage.dtype)
    load_amp.wait()
    for c in range(n_cd):
        stage[c, :, :width] = amp[:, c, :]
    for s in both:
        held[0, 0, s] = stage[flip(cd, s)]

    pl.semaphore_wait(barrier, len(peers))

    def remote(src, dst, s, r, peer):
        return pltpu.make_async_remote_copy(
            src_ref=src, dst_ref=dst, send_sem=s, recv_sem=r,
            device_id=peer, device_id_type=MESH,
        )

    def whole(like, sem):
        pltpu.make_async_copy(like, like, sem).wait()

    def sums(k):
        return acc.at[k] if k else part_ref.at[0]

    def cols(q):
        return pl.ds(q * LANES, LANES)

    acopy = {
        (k, s): remote(
            stage.at[flip(cd, 2 * k + s)], held.at[0, k, s], sent.at[0], a_r.at[k, s], (flip(cd, 2 * k), ab)
        )
        for k in FAR
        for s in both
    }
    xcopy = {
        (k, s): remote(held.at[0, k, s], held.at[2, k, s], sent.at[1], x_r.at[k, s], (cd, flip(ab, 2)))
        for k in range(n_z)
        for s in both
    }
    ccopy = {
        (r, k, s): remote(
            held.at[r, k, s], held.at[r + 1, k, s], sent.at[2], c_r.at[k], (cd, flip(ab, 1))
        )
        for r in (0, 2)
        for k in range(n_z)
        for s in both
    }
    deep = lent.shape[1]
    lend = {
        q: remote(mine.at[q, deep:], lent.at[q], sent.at[7], l_r.at[q], (cd, flip(ab, 1)))
        for q in range(pieces)
    }
    ycopy = {
        q: remote(mine.at[q, :deep], other.at[q, :deep], sent.at[3], y_r.at[q], (flip(cd, 1), ab))
        for q in range(pieces)
    }
    lcopy = {
        q: remote(lent.at[q], other.at[q, deep:], sent.at[3], y_r.at[q], (flip(cd, 1), flip(ab, 1)))
        for q in range(pieces)
    }
    zcopy = {
        (k, q): remote(
            acc.at[k, :, cols(q)], part_ref.at[k, :, cols(q)], sent.at[3 + k], z_r.at[k], (flip(cd, 2 * k), ab)
        )
        for k in FAR
        for q in range(pieces)
        if k < 3 or q >= VIA
    }
    hcopy = {
        q: remote(acc.at[3, :, cols(q)], near.at[q], sent.at[8], h_r.at[q], (flip(cd, 2), ab)) for q in range(VIA)
    }
    for s in both:
        xcopy[0, s].start()
        ccopy[0, 0, s].start()
    for k in FAR:
        for s in both:
            acopy[k, s].start()
    core = lax.rem(ab, 2)
    whole(mine, local_sem.at[1])
    ycopy[0].start()
    for q in range(pieces):
        lend[q].start()

    @pl.when(core == 0)
    def _():
        for q in range(pieces):
            if q:
                ycopy[q].start()
            lend[q].wait_recv()
            lcopy[q].start()

    @pl.when(core == 1)
    def _():
        for q in range(pieces):
            lend[q].wait_recv()
            lcopy[q].start()
            if q:
                ycopy[q].start()

    for s in both:
        slab[s, :, width:, :] = jnp.zeros((n_ab, wide - width, columns), slab.dtype)
    for j in range(n_ab):
        for q in range(pieces):
            slab[0, j, :width, q * LANES : (q + 1) * LANES] = mine[q, j * width : (j + 1) * width, :]

    def arrive(k):
        for s in both:
            acopy[k, s].wait_recv()
            xcopy[k, s].start()
            ccopy[0, k, s].start()

    def relay(k):
        for s in both:
            xcopy[k, s].wait_recv()
            ccopy[2, k, s].start()

    def product(k):
        whole(held.at[0:2, k], c_r.at[k])
        total = jnp.dot(held[0, k, 0], slab[0, ab], preferred_element_type=jnp.float32)
        for r in range(1, n_ab):
            total += jnp.dot(held[r, k, 0], slab[0, flip(ab, r)], preferred_element_type=jnp.float32)
        sums(k)[...] = total

    def piece(q):
        whole(other.at[q], y_r.at[q])
        here = slice(q * LANES, (q + 1) * LANES)
        for j in range(n_ab):
            slab[1, j, :width, here] = other[q, j * width : (j + 1) * width, :]

    def finish(kq):
        k, q = kq
        here = slice(q * LANES, (q + 1) * LANES)
        total = sums(k)[:, here]
        for r in range(n_ab):
            total += jnp.dot(held[r, k, 1], slab[1, flip(ab, r), :, here], preferred_element_type=jnp.float32)
        sums(k)[:, here] = total
        if k == 3 and q < VIA:
            hcopy[q].start()
        elif k == 1 or k and q >= VIA:
            zcopy[k, q].start()

    def pass_on(q):
        h = slice(q * LANES, (q + 1) * LANES)
        hcopy[q].wait_recv()
        acc[2, :, h] += near[q]
        zcopy[2, q].start()

    def pass_first(q):
        @pl.when(core == 1)
        def _():
            pass_on(q)

    def pass_later(q):
        @pl.when(core == 0)
        def _():
            pass_on(q)

    part_ref[3, :, : VIA * LANES] = jnp.zeros((rows, VIA * LANES), part_ref.dtype)
    act = {"a": arrive, "r": relay, "p": product, "y": piece, "f": finish, "h": pass_on, "i": pass_first, "j": pass_later}
    for what, k in PLAN:
        act[what](k)
    whole(held.at[0, 1:], sent.at[0])
    whole(near, sent.at[8])
    whole(held.at[0], sent.at[1])
    whole(held.at[0:2], sent.at[2])
    whole(other, sent.at[3])
    whole(lent, sent.at[7])
    for k in FAR:
        direct = acc.at[k, :, VIA * LANES :] if k == 3 else acc.at[k]
        whole(direct, sent.at[3 + k])
        whole(direct, z_r.at[k])


def by_kernel(amplitudes, integrals, n_ab):
    rows, n_cd, width = amplitudes.shape
    columns = integrals.shape[2]
    wide = -(-width // LANES) * LANES
    n_z = n_cd // 2
    pieces = columns // LANES
    dma = pltpu.SemaphoreType.DMA
    parts = pl.pallas_call(
        kernel,
        out_shape=pltpu.VMEM((n_z, rows, columns), jnp.float32),
        in_specs=[pl.BlockSpec(memory_space=pltpu.HBM)] * 2,
        out_specs=pl.BlockSpec(memory_space=pltpu.VMEM),
        scratch_shapes=[
            pltpu.VMEM((n_cd, rows, wide), amplitudes.dtype),
            pltpu.VMEM((n_ab, n_z, 2, rows, wide), amplitudes.dtype),
            pltpu.VMEM((2, n_ab, wide, columns), integrals.dtype),
            pltpu.VMEM((n_z, rows, columns), jnp.float32),
            pltpu.VMEM(amplitudes.shape, amplitudes.dtype),
            pltpu.VMEM((pieces, integrals.shape[1], LANES), integrals.dtype),
            pltpu.VMEM((pieces, integrals.shape[1], LANES), integrals.dtype),
            pltpu.VMEM((pieces, integrals.shape[1] // 2, LANES), integrals.dtype),
            dma((9,)), dma((n_z, 2)), dma((n_z, 2)), dma((n_z,)), dma((pieces,)), dma((pieces,)), dma((n_z,)), dma((VIA,)), pltpu.VMEM((VIA, rows, LANES), jnp.float32),
            dma((2,)),
        ],
        compiler_params=pltpu.CompilerParams(
            collective_id=0, has_side_effects=True, vmem_limit_bytes=32 * 1024 * 1024
        ),
    )(
        pltpu.with_memory_space_constraint(amplitudes, pltpu.HBM),
        pltpu.with_memory_space_constraint(integrals.reshape(integrals.shape[1], columns), pltpu.HBM),
    )
    return jnp.sum(parts, axis=0)


def by_collectives(amplitudes, integrals):
    c_local, depth, columns = integrals.shape
    mine = lax.all_to_all(amplitudes, "cd", split_axis=1, concat_axis=0, tiled=True)
    complete = lax.all_gather(mine, "ab", axis=2, tiled=True)
    flat = complete.reshape(complete.shape[0], c_local * depth)
    slab = integrals.reshape(c_local * depth, columns)
    partial = jnp.dot(flat, slab, preferred_element_type=jnp.float32)
    return lax.psum_scatter(partial, "cd", scatter_dimension=0, tiled=True)


def on_device(n_cd, n_ab, amplitudes, integrals):
    rows = amplitudes.shape[0]
    columns = integrals.shape[2]
    if n_cd == 8 and n_ab == 4 and integrals.shape[0] == 1 and rows % 16 == 0 and columns % LANES == 0 and integrals.shape[1] % 32 == 0:
        return by_kernel(amplitudes, integrals, n_ab)
    return by_collectives(amplitudes, integrals)


def solution(mesh):
    specs = (P("cd", None, "ab"), P("cd", None, "ab"))
    return jax.shard_map(
        functools.partial(on_device, mesh.shape["cd"], mesh.shape["ab"]),
        mesh=mesh, in_specs=specs, out_specs=P("cd", "ab"), check_vma=False,
    )
```

```python
import functools

import jax
import jax.numpy as jnp
from jax import lax
from jax.experimental import pallas as pl
from jax.experimental.pallas import tpu as pltpu
from jax.sharding import PartitionSpec as P

MESH = pl.DeviceIdType.MESH
LANES = 128
VIA = 1
FAR = (1, 3, 2)
PLAN = (
    ("a", 1), ("a", 3), ("r", 0), ("r", 1), ("a", 2), ("p", 1), ("y", 0), ("f", (1, 0)), ("r", 3), ("p", 0), ("r", 2), ("p", 3), ("f", (3, 0)), ("p", 2), ("f", (2, 0)), ("y", 1), ("f", (3, 1)), ("f", (2, 1)), ("f", (1, 1)), ("f", (0, 0)), ("f", (0, 1)), ("i", 0), ("y", 2), ("f", (3, 2)), ("f", (2, 2)), ("f", (1, 2)), ("f", (0, 2)), ("j", 0), ("y", 3), ("f", (2, 3)), ("f", (3, 3)), ("f", (1, 3)), ("f", (0, 3)),
)


def flip(index, bits):
    out = index
    bit = 1
    while bit <= bits:
        if bits & bit:
            out = out + bit - 2 * bit * (lax.div(index, bit) % 2)
        bit *= 2
    return out


def kernel(
    amp_ref, int_ref, out_ref, part_ref, stage, held, slab, acc, amp, mine, other, lent,
    sent, a_r, x_r, c_r, y_r, l_r, z_r, h_r, near, local_sem,
):
    cd = lax.axis_index("cd")
    ab = lax.axis_index("ab")
    rows, n_cd, width = amp_ref.shape
    wide = stage.shape[2]
    n_ab = slab.shape[1]
    n_z = held.shape[1]
    columns = int_ref.shape[1]
    pieces = columns // LANES
    both = (0, 1)

    load_amp = pltpu.make_async_copy(amp_ref, amp, local_sem.at[0])
    load_int = [
        pltpu.make_async_copy(int_ref.at[:, pl.ds(q * LANES, LANES)], mine.at[q], local_sem.at[1])
        for q in range(pieces)
    ]
    load_amp.start()
    for q in range(pieces):
        load_int[q].start()
    peers = [(flip(cd, k), ab) for k in (1, 2, 4, 6)]
    peers += [(cd, flip(ab, 1)), (cd, flip(ab, 2)), (flip(cd, 1), flip(ab, 1))]
    barrier = pltpu.get_barrier_semaphore()
    for peer in peers:
        pl.semaphore_signal(barrier, inc=1, device_id=peer, device_id_type=MESH)

    stage[:, :, width:] = jnp.zeros((n_cd, rows, wide - width), stage.dtype)
    load_amp.wait()
    for c in range(n_cd):
        stage[c, :, :width] = amp[:, c, :]
    for s in both:
        held[0, 0, s] = stage[flip(cd, s)]

    pl.semaphore_wait(barrier, len(peers))

    def remote(src, dst, s, r, peer):
        return pltpu.make_async_remote_copy(
            src_ref=src, dst_ref=dst, send_sem=s, recv_sem=r,
            device_id=peer, device_id_type=MESH,
        )

    def whole(like, sem):
        pltpu.make_async_copy(like, like, sem).wait()

    def sums(k):
        return acc.at[k] if k else part_ref.at[0]

    def cols(q):
        return pl.ds(q * LANES, LANES)

    acopy = {
        (k, s): remote(
            stage.at[flip(cd, 2 * k + s)], held.at[0, k, s], sent.at[0], a_r.at[k - 1, s], (flip(cd, 2 * k), ab)
        )
        for k in FAR
        for s in both
    }
    xcopy = {
        (k, s): remote(held.at[0, k, s], held.at[2, k, s], sent.at[1], x_r.at[k, s], (cd, flip(ab, 2)))
        for k in range(n_z)
        for s in both
    }
    ccopy = {
        (r, k, s): remote(
            held.at[r, k, s], held.at[r + 1, k, s], sent.at[2], c_r.at[k], (cd, flip(ab, 1))
        )
        for r in (0, 2)
        for k in range(n_z)
        for s in both
    }
    deep = lent.shape[1]
    lend = {
        q: remote(mine.at[q, deep:], lent.at[q], sent.at[5], l_r.at[q], (cd, flip(ab, 1)))
        for q in range(pieces)
    }
    ycopy = {
        q: remote(mine.at[q, :deep], other.at[q, :deep], sent.at[3], y_r.at[q], (flip(cd, 1), ab))
        for q in range(pieces)
    }
    lcopy = {
        q: remote(lent.at[q], other.at[q, deep:], sent.at[3], y_r.at[q], (flip(cd, 1), flip(ab, 1)))
        for q in range(pieces)
    }
    zcopy = {
        (k, q): remote(
            acc.at[k, :, cols(q)], part_ref.at[k, :, cols(q)], sent.at[4], z_r.at[k - 1, q // (pieces - 1)], (flip(cd, 2 * k), ab)
        )
        for k in FAR
        for q in range(pieces)
        if k < 3 or q >= VIA
    }
    hcopy = {
        q: remote(acc.at[3, :, cols(q)], near.at[q], sent.at[4], h_r.at[q], (flip(cd, 2), ab)) for q in range(VIA)
    }
    for s in both:
        xcopy[0, s].start()
        ccopy[0, 0, s].start()
    for k in FAR:
        for s in both:
            acopy[k, s].start()
    core = lax.rem(ab, 2)
    whole(mine, local_sem.at[1])
    ycopy[0].start()
    for q in range(pieces):
        lend[q].start()

    @pl.when(core == 0)
    def _():
        for q in range(pieces):
            if q:
                ycopy[q].start()
            lend[q].wait_recv()
            lcopy[q].start()

    @pl.when(core == 1)
    def _():
        for q in range(pieces):
            lend[q].wait_recv()
            lcopy[q].start()
            if q:
                ycopy[q].start()

    for s in both:
        slab[s, :, width:, :] = jnp.zeros((n_ab, wide - width, columns), slab.dtype)
    for j in range(n_ab):
        for q in range(pieces):
            slab[0, j, :width, q * LANES : (q + 1) * LANES] = mine[q, j * width : (j + 1) * width, :]

    def arrive(k):
        for s in both:
            acopy[k, s].wait_recv()
            xcopy[k, s].start()
            ccopy[0, k, s].start()

    def relay(k):
        for s in both:
            xcopy[k, s].wait_recv()
            ccopy[2, k, s].start()

    def product(k):
        whole(held.at[0:2, k], c_r.at[k])
        total = jnp.dot(held[0, k, 0], slab[0, ab], preferred_element_type=jnp.float32)
        for r in range(1, n_ab):
            total += jnp.dot(held[r, k, 0], slab[0, flip(ab, r)], preferred_element_type=jnp.float32)
        sums(k)[...] = total

    def piece(q):
        whole(other.at[q], y_r.at[q])
        here = slice(q * LANES, (q + 1) * LANES)
        for j in range(n_ab):
            slab[1, j, :width, here] = other[q, j * width : (j + 1) * width, :]

    def finish(kq):
        k, q = kq
        here = slice(q * LANES, (q + 1) * LANES)
        total = sums(k)[:, here]
        for r in range(n_ab):
            total += jnp.dot(held[r, k, 1], slab[1, flip(ab, r), :, here], preferred_element_type=jnp.float32)
        sums(k)[:, here] = total
        if k == 3 and q < VIA:
            hcopy[q].start()
        elif k == 1 or k and q >= VIA:
            zcopy[k, q].start()

    def pass_on(q):
        h = slice(q * LANES, (q + 1) * LANES)
        hcopy[q].wait_recv()
        acc[2, :, h] += near[q]
        zcopy[2, q].start()

    def pass_first(q):
        @pl.when(core == 1)
        def _():
            pass_on(q)

    def pass_later(q):
        @pl.when(core == 0)
        def _():
            pass_on(q)

    part_ref[3, :, : VIA * LANES] = jnp.zeros((rows, VIA * LANES), part_ref.dtype)
    act = {"a": arrive, "r": relay, "p": product, "y": piece, "f": finish, "h": pass_on, "i": pass_first, "j": pass_later}
    for what, k in PLAN:
        act[what](k)
    whole(held.at[0, 1:], sent.at[0])
    whole(held.at[0], sent.at[1])
    whole(held.at[0:2], sent.at[2])
    whole(other, sent.at[3])
    whole(lent, sent.at[5])
    whole(acc.at[1:], sent.at[4])
    early = (pieces - 1) * LANES
    for first, last, n in ((0, early, 0), (early, columns, 1)):
        for k in FAR:
            begin = VIA * LANES if k == 3 and not n else first
            whole(acc.at[k, :, begin:last], z_r.at[k - 1, n])
        h = slice(first, last)
        out_ref[:, h] = (part_ref[0, :, h] + part_ref[1, :, h]) + (part_ref[2, :, h] + part_ref[3, :, h])


def by_kernel(amplitudes, integrals, n_ab):
    rows, n_cd, width = amplitudes.shape
    columns = integrals.shape[2]
    wide = -(-width // LANES) * LANES
    n_z = n_cd // 2
    pieces = columns // LANES
    dma = pltpu.SemaphoreType.DMA
    return pl.pallas_call(
        kernel,
        out_shape=pltpu.VMEM((rows, columns), jnp.float32),
        in_specs=[pl.BlockSpec(memory_space=pltpu.HBM)] * 2,
        out_specs=pl.BlockSpec(memory_space=pltpu.VMEM),
        scratch_shapes=[
            pltpu.VMEM((n_z, rows, columns), jnp.float32),
            pltpu.VMEM((n_cd, rows, wide), amplitudes.dtype),
            pltpu.VMEM((n_ab, n_z, 2, rows, wide), amplitudes.dtype),
            pltpu.VMEM((2, n_ab, wide, columns), integrals.dtype),
            pltpu.VMEM((n_z, rows, columns), jnp.float32),
            pltpu.VMEM(amplitudes.shape, amplitudes.dtype),
            pltpu.VMEM((pieces, integrals.shape[1], LANES), integrals.dtype),
            pltpu.VMEM((pieces, integrals.shape[1], LANES), integrals.dtype),
            pltpu.VMEM((pieces, integrals.shape[1] // 2, LANES), integrals.dtype),
            dma((6,)), dma((n_z - 1, 2)), dma((n_z, 2)), dma((n_z,)), dma((pieces,)), dma((pieces,)), dma((n_z - 1, 2)), dma((VIA,)), pltpu.VMEM((VIA, rows, LANES), jnp.float32),
            dma((2,)),
        ],
        compiler_params=pltpu.CompilerParams(
            collective_id=0, has_side_effects=True, vmem_limit_bytes=32 * 1024 * 1024
        ),
    )(
        pltpu.with_memory_space_constraint(amplitudes, pltpu.HBM),
        pltpu.with_memory_space_constraint(integrals.reshape(integrals.shape[1], columns), pltpu.HBM),
    )


def by_collectives(amplitudes, integrals):
    c_local, depth, columns = integrals.shape
    mine = lax.all_to_all(amplitudes, "cd", split_axis=1, concat_axis=0, tiled=True)
    complete = lax.all_gather(mine, "ab", axis=2, tiled=True)
    flat = complete.reshape(complete.shape[0], c_local * depth)
    slab = integrals.reshape(c_local * depth, columns)
    partial = jnp.dot(flat, slab, preferred_element_type=jnp.float32)
    return lax.psum_scatter(partial, "cd", scatter_dimension=0, tiled=True)


def on_device(n_cd, n_ab, amplitudes, integrals):
    rows = amplitudes.shape[0]
    columns = integrals.shape[2]
    if n_cd == 8 and n_ab == 4 and integrals.shape[0] == 1 and rows % 16 == 0 and columns % LANES == 0 and integrals.shape[1] % 32 == 0:
        return by_kernel(amplitudes, integrals, n_ab)
    return by_collectives(amplitudes, integrals)


def solution(mesh):
    specs = (P("cd", None, "ab"), P("cd", None, "ab"))
    return jax.shard_map(
        functools.partial(on_device, mesh.shape["cd"], mesh.shape["ab"]),
        mesh=mesh, in_specs=specs, out_specs=P("cd", "ab"), check_vma=False,
    )
```
